32 devices in a mesh: groups: 2 (over x), lon: 16 (over z, y, core).
Axes of the slice: x: 2, y: 2, z: 4, core: 2. Of those that a mesh axis runs over, the one named last changes fastest.
Arguments:
- fields: bfloat16 [32, 256, 512], P(None, ('groups', 'lon')), parts along dimension 1, may hold values from -6 to 6
- order: int32 [16, 256], P('lon'), may hold values from 0 to 255, each once within a row
- resets: int32 [16, 256], P('lon'), may hold values 0 or 1
- land: int32 [32, 128], P(None, 'lon'), may hold values 0 or 1
- xbc_weight: bfloat16 [2, 512, 1280], replicated, may hold values from -0.25 to 0.25
- gate_weight: bfloat16 [2, 512, 1024], replicated, may hold values from -0.25 to 0.25
- step_weight: bfloat16 [2, 512, 16], replicated, may hold values from -0.25 to 0.25
- conv_weight: float32 [2, 3, 3, 1280], replicated, may hold values from -1 to 1
- land_shift: float32 [2, 16], replicated, may hold values from 0.5 to 2
- rates: float32 [2, 16], replicated, may hold values from 4.8828124e-06 to 0.03
- keeps: float32 [2, 16], replicated, may hold values from 0.5 to 0.8
- skip_gain: float32 [2, 16], replicated, may hold values from 0.5 to 1.5
- norm_gain: float32 [2, 1024], replicated, may hold values from 0.1 to 1.9
- out_weight: bfloat16 [2, 1024, 512], replicated, may hold values from -0.1875 to 0.1875
Outputs:
- forecast: bfloat16 [32, 256, 512], P(None, ('groups', 'lon')), parts along dimension 1
The draws below stay inside these ranges and needn't reach their ends.
There are 2 independent parts, one for each index of `groups`. The reference program is written for one: setup_inputs(seed, part) draws one part's arguments, and reference() takes and returns one part's arrays. A program takes and returns all parts, laid end to end along the dimension named above; an argument that names none is the same for every part. Nothing has to cross between parts.
Inputs may be any that keep to these rules, and one draw needn't show every extreme that they name: `order`: each row lists every cell index of one tile once.
All inputs are finite; a program needn't handle non-finite values. No bound on the sum of `resets` or of `land` on one device may be relied on, other than what follows from the above.
Results may differ from the reference program's by a relative error of at most 0.008.
Values may be sent and summed in bfloat16 or wider, within the bound.
A program may use at most 192 MiB of HBM per device.

```python
import math
import jax
import jax.numpy as jnp
from jax import lax

D = 512
H = 16
P_SIZE = 64
N = 128
E = 1024
Q = 128
LAYERS = 2
LAT = 32
LON_DEV = 8
CELLS = 256
TILES = 16
LON = 128


def with_ends(values, stream_key, least, largest):
    shape = values.shape
    spot = [jax.random.randint(jax.random.fold_in(stream_key, axis), (), 0, shape[axis]) for axis in range(len(shape))]
    values = values.at[tuple(spot)].set(least)
    longest = shape.index(max(shape))
    spot[longest] = (spot[longest] + 1) % shape[longest]
    return values.at[tuple(spot)].set(largest)


def steps_of(key, extent, split, low, top_value):
    level, own = 1.0, jax.random.fold_in(key, 6)
    for position, parts in split:
        heights = jnp.exp(jax.random.uniform(jax.random.fold_in(own, position), (parts,), jnp.float32, low / len(split), top_value / len(split)))
        level = level * jnp.repeat(heights, extent[position] // parts).reshape([-1 if axis == position else 1 for axis in range(len(extent))])
    return level


def scatter_about(stream_key, dims, scale, most, shards=(), held_as=jnp.bfloat16):
    values = jax.random.normal(stream_key, dims, jnp.float32) * scale
    if len(shards) > 0:
        values = steps_of(stream_key, dims, shards, -0.22, 0.18) * values
    return jnp.clip(values, min=-most, max=most).astype(held_as)


def setup_inputs(seed: int = 0, part: int = 0) -> dict:
    seeds = jax.random.split(jax.random.key(seed), 15)
    own_keys = jax.random.split(jax.random.fold_in(seeds[14], part), 15)
    return {
        "fields": scatter_about(own_keys[0], (LAT, LON, D), 1.0, 6.0, ((1, 16),)),
        "order": jax.vmap(lambda own: jax.random.permutation(own, CELLS))(jax.random.split(seeds[1], TILES)).reshape((TILES, CELLS)).astype(jnp.int32),
        "resets": with_ends((jax.random.randint(seeds[2], (TILES, CELLS), 0, CELLS * TILES) < 3).astype(jnp.int32), jax.random.fold_in(seeds[2], 1), 0, 1),
        "land": with_ends((jax.random.randint(seeds[3], (LAT, LON), 0, 3) < 1).astype(jnp.int32), jax.random.fold_in(seeds[3], 1), 0, 1),
        "xbc_weight": scatter_about(seeds[4], (LAYERS, D, E + 2 * N), D ** -0.5, 0.25),
        "gate_weight": scatter_about(seeds[5], (LAYERS, D, E), D ** -0.5, 0.25),
        "step_weight": scatter_about(seeds[6], (LAYERS, D, H), D ** -0.5, 0.25),
        "conv_weight": scatter_about(seeds[7], (LAYERS, 3, 3, E + 2 * N), 0.33, 1.0, (), jnp.float32),
        "land_shift": jnp.clip(jax.random.uniform(seeds[8], (LAYERS, H), jnp.float32, 0.5, 2.0), 0.5, 2.0),
        "rates": jnp.clip(jnp.exp(jax.random.uniform(seeds[9], (LAYERS, H), jnp.float32, math.log(4.882812390860636e-06), math.log(0.03))), 4.882812390860636e-06, 0.03),
        "keeps": jnp.clip(jax.random.uniform(seeds[10], (LAYERS, H), jnp.float32, 0.5, 0.8), 0.5, 0.8),
        "skip_gain": jnp.clip(jax.random.uniform(seeds[11], (LAYERS, H), jnp.float32, 0.5, 1.5), 0.5, 1.5),
        "norm_gain": jnp.clip(1.0 + 0.18 * jax.random.normal(seeds[12], (LAYERS, E), jnp.float32), 0.1, 1.9),
        "out_weight": scatter_about(seeds[13], (LAYERS, E, D), E ** -0.5, 0.1875),
    }


epsilon = 1e-05

def rms_round(values):
    return (values * lax.rsqrt(lax.optimization_barrier(jnp.mean(values * values, axis=-1, keepdims=True)) + epsilon)).astype(jnp.bfloat16)

def to_tiles(grid):
    depth = grid.shape[-1]
    return grid.reshape(LAT, TILES, LON_DEV, depth).transpose(1, 0, 2, 3).reshape(TILES, LAT * LON_DEV, depth)

def from_tiles(tiled):
    depth = tiled.shape[-1]
    return tiled.reshape(TILES, LAT, LON_DEV, depth).transpose(1, 0, 2, 3).reshape(LAT, TILES * LON_DEV, depth)

def tile_pass(state, act_seq, dt_seq, reset_seq, rate, keep, skip):
    count_cells = act_seq.shape[0]
    blocks = count_cells // Q
    inputs = act_seq[:, :E].astype(jnp.float32).reshape(blocks, Q, H, P_SIZE)
    in_maps = act_seq[:, E:E + N].astype(jnp.float32).reshape(blocks, Q, N)
    out_maps = act_seq[:, E + N:].astype(jnp.float32).reshape(blocks, Q, N)
    log_step = -rate[None, :] * dt_seq + reset_seq[:, None] * jnp.log(keep)[None, :]
    log_cum = jnp.cumsum(log_step.reshape(blocks, Q, H), axis=1)
    steps_blk = dt_seq.reshape(blocks, Q, H)
    causal = jnp.arange(Q)[:, None] >= jnp.arange(Q)[None, :]

    def one_block(carry, pieces):
        values, bmap, cmap, cum, steps_here = pieces
        scores = jnp.dot(cmap, bmap.T, precision=lax.Precision.HIGHEST)
        cum_h = cum.T
        spread = cum_h[:, :, None] - cum_h[:, None, :]
        decay = jnp.where(causal[None], jnp.exp(jnp.where(causal[None], spread, 0.0)), 0.0)
        mix = (scores[None] * decay * steps_here.T[:, None, :]).astype(jnp.bfloat16).astype(jnp.float32)
        within = jnp.einsum('hqs,shp->qhp', mix, values)
        outside = jnp.exp(cum)[:, :, None] * jnp.einsum('qn,hpn->qhp', cmap, carry, precision=lax.Precision.HIGHEST)
        result = within + outside + skip[None, :, None] * values
        weight = jnp.exp(cum[-1:, :] - cum) * steps_here
        weighted = (values * weight[:, :, None]).astype(jnp.bfloat16).astype(jnp.float32)
        added = jnp.einsum('qhp,qn->hpn', weighted, bmap)
        carry = jnp.exp(cum[-1, :])[:, None, None] * carry + added
        return (carry, result)
    state, results = lax.scan(one_block, state, (inputs, in_maps, out_maps, log_cum, steps_blk))
    return (state, results.reshape(count_cells, E))

def reference(fields, order, resets, land, xbc_weight, gate_weight, step_weight, conv_weight, land_shift, rates, keeps, skip_gain, norm_gain, out_weight):
    stream = fields
    width = fields.shape[2]
    count_cells = LAT * LON_DEV
    for block_index in range(LAYERS):
        normed = rms_round(stream.astype(jnp.float32))
        flat = normed.reshape(-1, width)
        mapped = jnp.dot(flat, xbc_weight[block_index], preferred_element_type=jnp.float32).astype(jnp.bfloat16).reshape(LAT, LON, -1)
        gate = jnp.dot(flat, gate_weight[block_index], preferred_element_type=jnp.float32).astype(jnp.bfloat16).reshape(LAT, LON, -1)
        raw_step = jnp.dot(flat, step_weight[block_index], preferred_element_type=jnp.float32).reshape(LAT, LON, -1)
        steps_grid = jax.nn.softplus(raw_step + land.astype(jnp.float32)[:, :, None] * land_shift[block_index][None, None, :])
        wrapped = jnp.concatenate([mapped[:, -1:], mapped, mapped[:, :1]], axis=1)
        padded = jnp.pad(wrapped, ((1, 1), (0, 0), (0, 0)))
        total = jnp.zeros(mapped.shape, jnp.float32)
        for row_off in range(3):
            for col_off in range(3):
                total = total + padded[row_off:row_off + LAT, col_off:col_off + LON].astype(jnp.float32) * conv_weight[block_index, row_off, col_off]
        act = jax.nn.silu(total).astype(jnp.bfloat16)
        picks = order[:, :, None]
        act_seq = jnp.take_along_axis(to_tiles(act), picks, axis=1)
        gate_seq = jnp.take_along_axis(to_tiles(gate), picks, axis=1)
        dt_seq = jnp.take_along_axis(to_tiles(steps_grid), picks, axis=1)
        reset_seq = resets.astype(jnp.float32)

        def over_tiles(state, pieces):
            return tile_pass(state, pieces[0], pieces[1], pieces[2], rates[block_index], keeps[block_index], skip_gain[block_index])
        start = jnp.zeros((H, P_SIZE, N), jnp.float32)
        _, outputs = lax.scan(over_tiles, start, (act_seq, dt_seq, reset_seq))
        gated = outputs * jax.nn.silu(gate_seq.astype(jnp.float32))
        gated = gated * lax.rsqrt(lax.optimization_barrier(jnp.mean(gated * gated, axis=-1, keepdims=True)) + epsilon) * norm_gain[block_index]
        gated = gated.astype(jnp.bfloat16)
        projected = jnp.dot(gated.reshape(-1, E), out_weight[block_index], preferred_element_type=jnp.float32).reshape(TILES, count_cells, width)
        placed = jax.vmap(lambda rows, where: jnp.zeros((count_cells, width), jnp.float32).at[where].set(rows))(projected, order)
        stream = (stream.astype(jnp.float32) + from_tiles(placed)).astype(jnp.bfloat16)
    return stream
```

```python
import functools

import jax
import jax.numpy as jnp
from jax import lax
from jax.experimental import pallas as pl
from jax.experimental.pallas import tpu as pltpu
from jax.sharding import PartitionSpec as P

H = 16
P_SIZE = 64
N = 128
E = 1024
Q = 128
LAYERS = 2
PAIRS = H // 2

epsilon = 1e-05
bf16 = jnp.bfloat16
f32 = jnp.float32


def mm(a, b):
    return jnp.dot(a, b, preferred_element_type=f32)


def split(values):
    high = values.astype(bf16)
    low = (values - high.astype(f32)).astype(bf16)
    return high, low


def of_layer(ref, layer):
    return jnp.where(layer == 0, ref[0:1], ref[1:2])


def iota(shape, dim):
    return lax.broadcasted_iota(jnp.int32, shape, dim)


def kernel(
    tiles,
    chunks,
    width,
    fields,
    order,
    resets,
    land,
    xbc_w,
    gate_w,
    step_w,
    conv_w,
    shift,
    rates,
    keeps,
    skip,
    gain,
    out_w,
    out,
    stream,
    perm,
    perm_t,
    normed,
    mapped,
    act,
    seq,
    normed_seq,
    gates,
    lt,
    dtt,
    y,
    wide,
    added0,
    halo_out,
    halo_in,
    s_out,
    s_in,
    d_out,
    d_in,
    d_wide,
    p_out,
    p_in,
    halo_send,
    halo_recv,
    s_send,
    s_recv,
    d_send,
    d_recv,
    p_send,
    p_recv,
):
    lat, across, channels = fields.shape
    cells = lat * across
    per_row = E // width
    me = lax.axis_index("lon")
    right, left = lax.rem(me + 1, tiles), lax.rem(me + tiles - 1, tiles)

    barrier = pltpu.get_barrier_semaphore()

    @pl.loop(1, tiles)
    def _(step):
        pl.semaphore_signal(
            barrier,
            inc=1,
            device_id={"lon": lax.rem(me + step, tiles)},
            device_id_type=pl.DeviceIdType.MESH,
        )

    perm_f = (order[...] == iota((cells, cells), 0)).astype(f32)
    perm_t[...] = perm_f.astype(bf16)
    perm_s = perm_f.T
    perm[...] = perm_s.astype(bf16)
    land_seq = jnp.sum(perm_s * land[...].astype(f32), axis=1, keepdims=True)
    rows, cols = iota((cells, cells), 0), iota((cells, cells), 1)
    reset_col = jnp.sum(
        jnp.where(rows == cols, resets[...].astype(f32), 0.0), axis=1, keepdims=True
    )
    stream[...] = fields[...].astype(f32).reshape(cells, channels)

    pl.semaphore_wait(barrier, tiles - 1)

    def remote(src, dst, send, recv, peer):
        return pltpu.make_async_remote_copy(
            src_ref=src,
            dst_ref=dst,
            send_sem=send,
            recv_sem=recv,
            device_id={"lon": peer},
            device_id_type=pl.DeviceIdType.MESH,
        )

    @pl.loop(0, LAYERS)
    def _(layer):
        values = stream[...]
        norm = (
            values * lax.rsqrt(jnp.mean(values * values, axis=-1, keepdims=True) + epsilon)
        ).astype(bf16)
        normed[...] = norm
        mapped_here = mm(norm, xbc_w[layer]).astype(bf16)
        mapped[...] = mapped_here

        edge_rows, edge_cols = iota((lat, cells), 0), iota((lat, cells), 1)
        first = (edge_cols == edge_rows * across).astype(f32).astype(bf16)
        last = (edge_cols == edge_rows * across + across - 1).astype(f32).astype(bf16)
        halo_out[0] = mm(first, mapped_here).astype(bf16)
        halo_out[1] = mm(last, mapped_here).astype(bf16)
        to_left = remote(
            halo_out.at[0], halo_in.at[layer, 1], halo_send.at[0], halo_recv.at[layer, 1], left
        )
        to_right = remote(
            halo_out.at[1], halo_in.at[layer, 0], halo_send.at[1], halo_recv.at[layer, 0], right
        )
        to_left.start()
        to_right.start()

        norm_seq = mm(perm[...], norm).astype(bf16)
        normed_seq[...] = norm_seq
        raw = mm(norm_seq, step_w[layer]) + land_seq * of_layer(shift, layer)
        dt = jnp.maximum(raw, 0.0) + jnp.log1p(jnp.exp(-jnp.abs(raw)))
        log_step = -of_layer(rates, layer) * dt + reset_col * jnp.log(of_layer(keeps, layer))
        lower = ((rows >= cols) & (rows // Q == cols // Q)).astype(f32)
        cum = jnp.dot(
            lower, log_step, precision=lax.Precision.HIGHEST, preferred_element_type=f32
        )
        cum0, cum1 = cum[Q - 1 : Q], cum[2 * Q - 1 : 2 * Q]
        second = iota((cells, H), 0) >= Q
        cum_t, dt_t = cum.T, dt.T
        for head in range(H):
            lt[head // 2, head % 2 : head % 2 + 1, :] = cum_t[head : head + 1]
            dtt[head // 2, head % 2 : head % 2 + 1, :] = dt_t[head : head + 1]
        d_out[...] = jnp.zeros_like(d_out)
        d_out[:, 0:H] = jnp.broadcast_to(jnp.exp(cum0 + cum1), (8, H))

        @pl.loop(1, tiles)
        def _(step):
            remote(
                d_out,
                d_in.at[layer, me],
                d_send.at[step],
                d_recv.at[layer, me],
                lax.rem(me + step, tiles),
            ).start()

        d_in[layer, me] = d_out[...]

        weight = jnp.exp(jnp.where(second, cum1, cum0) - cum) * dt
        since = jnp.exp(cum)
        since_tile = jnp.exp(jnp.where(second, cum + cum0, cum))
        spread = (iota((H, E), 0) == iota((H, E), 1) // P_SIZE).astype(f32).astype(bf16)
        for index, compact in enumerate((weight, since, since_tile)):
            high, low = split(compact)
            wide[index] = mm(high, spread) + mm(low, spread)
        skip_high, skip_low = split(jnp.broadcast_to(of_layer(skip, layer), (8, H)))
        skip_wide = (mm(skip_high, spread) + mm(skip_low, spread))[0:1]

        to_left.wait_recv()
        to_right.wait_recv()

        group = 256
        place_rows, place_cols = iota((cells, lat), 0), iota((cells, lat), 1)
        at_first = (place_rows == place_cols * across).astype(f32).astype(bf16)
        at_last = (place_rows == place_cols * across + across - 1).astype(f32).astype(bf16)

        @pl.loop(0, xbc_w.shape[2] // group)
        def _(part):
            lanes = pl.ds(pl.multiple_of(part * group, group), group)
            mid = mapped[:, lanes].astype(f32).reshape(lat, across, group)
            column = iota((lat, across, group), 1)
            before = jnp.where(column == 0, 0.0, pltpu.roll(mid, 1, 1)) + mm(
                at_first, halo_in[layer, 0, :, lanes]
            ).reshape(lat, across, group)
            after = jnp.where(column == across - 1, 0.0, pltpu.roll(mid, across - 1, 1)) + mm(
                at_last, halo_in[layer, 1, :, lanes]
            ).reshape(lat, across, group)
            total = None
            empty = jnp.zeros((1, across, group), f32)
            for row_off in range(3):
                line = None
                for col_off, moved in enumerate((before, mid, after)):
                    factor = conv_w[layer, row_off, pl.ds(col_off, 1), lanes]
                    term = moved * factor[None]
                    line = term if line is None else line + term
                if row_off == 0:
                    line = jnp.concatenate([empty, line[:-1]], axis=0)
                if row_off == 2:
                    line = jnp.concatenate([line[1:], empty], axis=0)
                total = line if total is None else total + line
            act[:, lanes] = (
                (total * (1.0 / (1.0 + jnp.exp(-total)))).reshape(cells, group).astype(bf16)
            )

        seq[...] = mm(perm[...], act[...]).astype(bf16)

        x0, x1 = seq[0:Q, 0:E].astype(f32), seq[Q:, 0:E].astype(f32)
        wx0 = (x0 * wide[0, 0:Q]).astype(bf16)
        wx1 = (x1 * wide[0, Q:]).astype(bf16)
        b0, b1 = seq[0:Q, E : E + N], seq[Q:, E : E + N]
        b0_t = b0.astype(f32).T.astype(bf16)
        b1_t = b1.astype(f32).T.astype(bf16)
        first_added = mm(b0_t, wx0)
        added0[...] = first_added.astype(bf16)
        summary = (first_added * wide[1, 2 * Q - 1 : 2 * Q] + mm(b1_t, wx1)).astype(bf16)
        for chunk in range(chunks):
            r, c = chunk // per_row * 16, chunk % per_row * width
            s_out[chunk] = summary[r : r + 16, c : c + width]

        @pl.loop(1, tiles)
        def _(step):
            peer = lax.rem(me + step, tiles)

            @pl.when(peer < chunks)
            def _():
                remote(
                    s_out.at[peer],
                    s_in.at[layer, me],
                    s_send.at[step],
                    s_recv.at[layer, me],
                    peer,
                ).start()

        scores = [
            lax.dot_general(
                seq[k * Q : (k + 1) * Q, E + N :],
                seq[k * Q : (k + 1) * Q, E : E + N],
                (((1,), (1,)), ((), ())),
                preferred_element_type=f32,
            )
            for k in range(2)
        ]
        causal = iota((Q, Q), 0) >= iota((Q, Q), 1)
        low_lanes = iota((Q, 2 * P_SIZE), 1) < P_SIZE

        def pair_step(pair, carry):
            lanes = pl.ds(pl.multiple_of(pair * 2 * P_SIZE, 2 * P_SIZE), 2 * P_SIZE)
            for k in range(2):
                span = slice(k * Q, (k + 1) * Q)
                mixes = []
                for side in range(2):
                    row = lt[pair, side : side + 1, span]
                    step_row = dtt[pair, side : side + 1, span]
                    here = jnp.broadcast_to(row, (Q, Q))
                    decay = jnp.exp(jnp.where(causal, here.T - here, -1e30))
                    mixes.append((carry[k] * decay * step_row).astype(bf16))
                pair_x = seq[span, lanes].astype(f32)
                both = jnp.concatenate(
                    [jnp.where(low_lanes, pair_x, 0.0), jnp.where(low_lanes, 0.0, pair_x)], axis=0
                ).astype(bf16)
                y[span, lanes] = mm(jnp.concatenate(mixes, axis=1), both)
            return carry

        lax.fori_loop(0, PAIRS // 2, pair_step, tuple(scores))

        @pl.loop(1, tiles)
        def _(step):
            source = lax.rem(me + tiles - step, tiles)
            remote(d_out, d_in.at[layer, source], d_send.at[step], d_recv.at[layer, source], left).wait()

        @pl.when(me < chunks)
        def _():
            s_in[layer, me] = s_out[me]
            offset = lax.rem(me, per_row) * (width // P_SIZE)
            pick = (
                (iota((N, width), 0) == iota((N, width), 1) // P_SIZE + offset)
                .astype(f32)
                .astype(bf16)
            )
            high, low = split(d_in[layer].reshape(tiles * 8, N))
            d_wide[...] = (mm(high, pick) + mm(low, pick)).reshape(tiles, 8, width)

            def tile_step(tile, state):
                p_out[tile] = state.astype(bf16)

                @pl.when(tile != me)
                def _():
                    remote(
                        p_out.at[tile],
                        p_in.at[layer, me],
                        p_send.at[tile],
                        p_recv.at[layer, me],
                        tile,
                    ).start()
                    remote(
                        s_out.at[0], s_in.at[layer, tile], s_send.at[0], s_recv.at[layer, tile], left
                    ).wait_recv()

                return state * d_wide[tile, 0:1, :] + s_in[layer, tile].astype(f32)

            lax.fori_loop(0, tiles, tile_step, jnp.zeros((16, width), f32))
            p_in[layer, me] = p_out[me]

        lax.fori_loop(PAIRS // 2, PAIRS, pair_step, tuple(scores))
        gate = mm(normed_seq[...], gate_w[layer]).astype(bf16).astype(f32)
        gates[...] = gate * (1.0 / (1.0 + jnp.exp(-gate)))
        y[...] += skip_wide * seq[:, 0:E].astype(f32)
        y[Q:, :] += wide[1, Q:] * mm(seq[Q:, E + N :], added0[...])

        @pl.loop(0, chunks)
        def _(source):
            @pl.when(source != me)
            def _():
                remote(
                    p_out.at[0], p_in.at[layer, source], p_send.at[0], p_recv.at[layer, source], left
                ).wait_recv()

        entering = jnp.concatenate(
            [
                jnp.concatenate([p_in[layer, r * per_row + c] for c in range(per_row)], axis=1)
                for r in range(N // 16)
            ],
            axis=0,
        )
        result = y[...] + wide[2] * mm(seq[:, E + N :], entering)
        gated = result * gates[...]
        gated = (
            gated
            * lax.rsqrt(jnp.mean(gated * gated, axis=-1, keepdims=True) + epsilon)
            * of_layer(gain, layer)
        ).astype(bf16)
        back = mm(perm_t[...], gated).astype(bf16)
        stream[...] = (stream[...] + mm(back, out_w[layer])).astype(bf16).astype(f32)

        to_left.wait_send()
        to_right.wait_send()

        @pl.loop(1, tiles)
        def _(step):
            peer = lax.rem(me + step, tiles)

            @pl.when(peer < chunks)
            def _():
                remote(
                    s_out.at[peer], s_in.at[layer, me], s_send.at[step], s_recv.at[layer, me], peer
                ).wait_send()

            @pl.when(me < chunks)
            def _():
                remote(
                    p_out.at[peer], p_in.at[layer, me], p_send.at[peer], p_recv.at[layer, me], peer
                ).wait_send()

    out[...] = stream[...].reshape(lat, across, channels).astype(bf16)


def shards(
    fields,
    order,
    resets,
    land,
    xbc_weight,
    gate_weight,
    step_weight,
    conv_weight,
    land_shift,
    rates,
    keeps,
    skip_gain,
    norm_gain,
    out_weight,
):
    tiles = lax.axis_size("lon")
    lat, across, channels = fields.shape
    cells = lat * across
    mapped_width = xbc_weight.shape[2]
    width = max(128, 8 * E // tiles)
    chunks = N // 16 * (E // width)
    dma = pltpu.SemaphoreType.DMA
    vmem = pltpu.VMEM
    return pl.pallas_call(
        functools.partial(kernel, tiles, chunks, width),
        out_shape=jax.ShapeDtypeStruct(fields.shape, bf16),
        in_specs=[pl.BlockSpec(memory_space=vmem)] * 14,
        out_specs=pl.BlockSpec(memory_space=vmem),
        scratch_shapes=[
            vmem((cells, channels), f32),
            vmem((cells, cells), bf16),
            vmem((cells, cells), bf16),
            vmem((cells, channels), bf16),
            vmem((cells, mapped_width), bf16),
            vmem((cells, mapped_width), bf16),
            vmem((cells, mapped_width), bf16),
            vmem((cells, channels), bf16),
            vmem((cells, E), f32),
            vmem((PAIRS, 2, cells), f32),
            vmem((PAIRS, 2, cells), f32),
            vmem((cells, E), f32),
            vmem((3, cells, E), f32),
            vmem((N, E), bf16),
            vmem((2, lat, mapped_width), bf16),
            vmem((LAYERS, 2, lat, mapped_width), bf16),
            vmem((chunks, 16, width), bf16),
            vmem((LAYERS, tiles, 16, width), bf16),
            vmem((8, N), f32),
            vmem((LAYERS, tiles, 8, N), f32),
            vmem((tiles, 8, width), f32),
            vmem((tiles, 16, width), bf16),
            vmem((LAYERS, chunks, 16, width), bf16),
            dma((2,)),
            dma((LAYERS, 2)),
            dma((tiles,)),
            dma((LAYERS, tiles)),
            dma((tiles,)),
            dma((LAYERS, tiles)),
            dma((tiles,)),
            dma((LAYERS, chunks)),
        ],
        compiler_params=pltpu.CompilerParams(
            collective_id=0, has_side_effects=True, vmem_limit_bytes=48 * 1024 * 1024
        ),
        cost_estimate=pl.CostEstimate(
            flops=2 * 10**9, bytes_accessed=8 * 10**6, transcendentals=3 * 10**6
        ),
    )(
        fields,
        order,
        resets,
        land.reshape(1, cells),
        xbc_weight,
        gate_weight,
        step_weight,
        conv_weight,
        land_shift,
        rates,
        keeps,
        skip_gain,
        norm_gain,
        out_weight,
    )


def solution(mesh):
    return jax.shard_map(
        shards,
        mesh=mesh,
        in_specs=(
            P(None, ("groups", "lon"), None),
            P("lon", None),
            P("lon", None),
            P(None, "lon"),
            P(),
            P(),
            P(),
            P(),
            P(),
            P(),
            P(),
            P(),
            P(),
            P(),
        ),
        out_specs=P(None, ("groups", "lon"), None),
        check_vma=False,
    )
```

```python
import functools

import jax
import jax.numpy as jnp
from jax import lax
from jax.experimental import pallas as pl
from jax.experimental.pallas import tpu as pltpu
from jax.sharding import PartitionSpec as P

H = 16
P_SIZE = 64
N = 128
E = 1024
Q = 128
LAYERS = 2
PAIRS = H // 2

epsilon = 1e-05
bf16 = jnp.bfloat16
f32 = jnp.float32


def mm(a, b):
    return jnp.dot(a, b, preferred_element_type=f32)


def split(values):
    high = values.astype(bf16)
    low = (values - high.astype(f32)).astype(bf16)
    return high, low


def of_layer(ref, layer):
    return jnp.where(layer == 0, ref[0:1], ref[1:2])


def iota(shape, dim):
    return lax.broadcasted_iota(jnp.int32, shape, dim)


def kernel(
    tiles,
    team,
    *refs,
):
    names = 14
    given, (out, *refs) = refs[:names], refs[names:]
    held, refs = refs[:names], refs[names:]
    (fields, order, resets, land, xbc_w, gate_w, step_w, conv_w) = held[:8]
    (shift, rates, keeps, skip, gain, out_w) = held[8:]
    (
    given_sem,
    weight_sem,
    stream,
    perm,
    perm_t,
    mapped,
    act,
    seq,
    normed_seq,
    gates,
    lt,
    dtt,
    y,
    wide,
    added0,
    halo_out,
    halo_in,
    s_out,
    s_in,
    t_out,
    t_in,
    rel,
    factors,
    d_out,
    d_in,
    d_wide,
    p_out,
    p_in,
    halo_send,
    halo_recv,
    s_send,
    s_recv,
    t_send,
    t_recv,
    d_send,
    d_recv,
    p_send,
    p_recv,
    ) = refs
    lat, across, channels = fields.shape
    cells = lat * across
    teams = tiles // team
    half = E // 2
    owned = N // team
    me = lax.axis_index("lon")
    my_team, place = me // team, me % team
    base = my_team * team
    right, left = lax.rem(me + 1, tiles), lax.rem(me + tiles - 1, tiles)

    big = {4: 0, 5: 1, 13: 2}

    def fetch(index):
        return pltpu.make_async_copy(given[index], held[index], given_sem.at[index])

    def fetch_weight(index, layer):
        return pltpu.make_async_copy(
            given[index].at[layer], held[index].at[layer], weight_sem.at[big[index], layer]
        )

    small = [index for index in range(names) if index not in big]
    early = (0, 1, 2, 3)
    for index in early:
        fetch(index).start()
    fetch_weight(4, 0).start()
    for index in small:
        if index not in early:
            fetch(index).start()
    for index, layer in ((5, 0), (13, 0), (4, 1), (5, 1), (13, 1)):
        fetch_weight(index, layer).start()

    barrier = pltpu.get_barrier_semaphore()

    @pl.loop(1, tiles)
    def _(step):
        pl.semaphore_signal(
            barrier,
            inc=1,
            device_id={"lon": lax.rem(me + step, tiles)},
            device_id_type=pl.DeviceIdType.MESH,
        )

    for index in early:
        fetch(index).wait()
    perm_f = (order[...] == iota((cells, cells), 0)).astype(f32)
    perm_t[...] = perm_f.astype(bf16)
    perm_s = perm_f.T
    perm[...] = perm_s.astype(bf16)
    at_row = (iota((cells, lat), 0) // across == iota((cells, lat), 1)).astype(f32).astype(bf16)
    land_of = lax.dot_general(
        at_row,
        land[...].astype(f32).astype(bf16),
        (((1,), (1,)), ((), ())),
        preferred_element_type=f32,
    )
    on_column = iota((cells, across), 0) % across == iota((cells, across), 1)
    land_of = jnp.where(on_column, land_of, 0.0).astype(bf16)
    land_seq = jnp.sum(mm(perm[...], land_of), axis=1, keepdims=True)
    rows, cols = iota((cells, cells), 0), iota((cells, cells), 1)
    reset_col = jnp.sum(
        jnp.where(rows == cols, resets[...].astype(f32), 0.0), axis=1, keepdims=True
    )
    stream[...] = fields[...].astype(f32).reshape(cells, channels)

    for index in small:
        if index not in early:
            fetch(index).wait()
    pl.semaphore_wait(barrier, tiles - 1)

    def remote(src, dst, send, recv, peer):
        return pltpu.make_async_remote_copy(
            src_ref=src,
            dst_ref=dst,
            send_sem=send,
            recv_sem=recv,
            device_id={"lon": peer},
            device_id_type=pl.DeviceIdType.MESH,
        )

    @pl.loop(0, LAYERS)
    def _(layer):
        values = stream[...]
        norm = (
            values * lax.rsqrt(jnp.mean(values * values, axis=-1, keepdims=True) + epsilon)
        ).astype(bf16)
        fetch_weight(4, layer).wait()
        mapped_here = mm(norm, xbc_w[layer]).astype(bf16)
        mapped[...] = mapped_here

        edge_rows, edge_cols = iota((lat, cells), 0), iota((lat, cells), 1)
        first = (edge_cols == edge_rows * across).astype(f32).astype(bf16)
        last = (edge_cols == edge_rows * across + across - 1).astype(f32).astype(bf16)
        halo_out[0] = mm(first, mapped_here).astype(bf16)
        halo_out[1] = mm(last, mapped_here).astype(bf16)
        to_left = remote(
            halo_out.at[0], halo_in.at[layer, 1], halo_send.at[0], halo_recv.at[layer, 1], left
        )
        to_right = remote(
            halo_out.at[1], halo_in.at[layer, 0], halo_send.at[1], halo_recv.at[layer, 0], right
        )
        to_left.start()
        to_right.start()

        norm_seq = mm(perm[...], norm).astype(bf16)
        normed_seq[...] = norm_seq
        raw = lax.dot_general(
            norm_seq, step_w[layer], (((1,), (1,)), ((), ())), preferred_element_type=f32
        ) + land_seq * of_layer(shift, layer)
        dt = jnp.maximum(raw, 0.0) + jnp.log1p(jnp.exp(-jnp.abs(raw)))
        log_step = -of_layer(rates, layer) * dt + reset_col * jnp.log(of_layer(keeps, layer))
        lower = ((rows >= cols) & (rows // Q == cols // Q)).astype(f32)
        cum = jnp.dot(
            lower, log_step, precision=lax.Precision.HIGHEST, preferred_element_type=f32
        )
        cum0, cum1 = cum[Q - 1 : Q], cum[2 * Q - 1 : 2 * Q]
        second = iota((cells, H), 0) >= Q
        cum_t, dt_t = cum.T, dt.T
        for head in range(H):
            lt[head // 2, head % 2 : head % 2 + 1, :] = cum_t[head : head + 1]
            dtt[head // 2, head % 2 : head % 2 + 1, :] = dt_t[head : head + 1]
        d_out[...] = jnp.zeros_like(d_out)
        d_out[:, 0:H] = jnp.broadcast_to(jnp.exp(cum0 + cum1), (8, H))

        @pl.loop(1, tiles)
        def _(step):
            remote(
                d_out,
                d_in.at[layer, me],
                d_send.at[step],
                d_recv.at[layer, me],
                lax.rem(me + step, tiles),
            ).start()

        d_in[layer, me] = d_out[...]

        weight = jnp.exp(jnp.where(second, cum1, cum0) - cum) * dt
        since = jnp.exp(cum)
        since_tile = jnp.exp(jnp.where(second, cum + cum0, cum))
        spread = (iota((H, E), 0) == iota((H, E), 1) // P_SIZE).astype(f32).astype(bf16)
        for index, compact in enumerate((weight, since, since_tile)):
            high, low = split(compact)
            wide[index] = mm(high, spread) + mm(low, spread)
        skip_high, skip_low = split(jnp.broadcast_to(of_layer(skip, layer), (8, H)))
        skip_wide = (mm(skip_high, spread) + mm(skip_low, spread))[0:1]

        to_left.wait_recv()
        to_right.wait_recv()

        group = 256
        place_rows, place_cols = iota((cells, lat), 0), iota((cells, lat), 1)
        at_first = (place_rows == place_cols * across).astype(f32).astype(bf16)
        at_last = (place_rows == place_cols * across + across - 1).astype(f32).astype(bf16)

        def filter_part(part):
            lanes = pl.ds(pl.multiple_of(part * group, group), group)
            mid = mapped[:, lanes].astype(f32).reshape(lat, across, group)
            column = iota((lat, across, group), 1)
            before = jnp.where(column == 0, 0.0, pltpu.roll(mid, 1, 1)) + mm(
                at_first, halo_in[layer, 0, :, lanes]
            ).reshape(lat, across, group)
            after = jnp.where(column == across - 1, 0.0, pltpu.roll(mid, across - 1, 1)) + mm(
                at_last, halo_in[layer, 1, :, lanes]
            ).reshape(lat, across, group)
            total = None
            empty = jnp.zeros((1, across, group), f32)
            for row_off in range(3):
                line = None
                for col_off, moved in enumerate((before, mid, after)):
                    factor = jnp.where(
                        layer == 0,
                        conv_w[row_off, col_off, 0:1, lanes],
                        conv_w[row_off, col_off, 1:2, lanes],
                    )
                    term = moved * factor[None]
                    line = term if line is None else line + term
                if row_off == 0:
                    line = jnp.concatenate([empty, line[:-1]], axis=0)
                if row_off == 2:
                    line = jnp.concatenate([line[1:], empty], axis=0)
                total = line if total is None else total + line
            act[:, lanes] = (
                (total * (1.0 / (1.0 + jnp.exp(-total)))).reshape(cells, group).astype(bf16)
            )

        pl.loop(E // group, xbc_w.shape[2] // group)(filter_part)
        seq[:, E:] = mm(perm[...], act[:, E:]).astype(bf16)
        b0_t = seq[0:Q, E : E + N].astype(f32).T.astype(bf16)
        b1_t = seq[Q:, E : E + N].astype(f32).T.astype(bf16)

        for part in range(2):
            lanes = slice(part * half, (part + 1) * half)
            pl.loop(part * (half // group), (part + 1) * (half // group))(filter_part)
            x_seq = mm(perm[...], act[:, lanes])
            seq[:, lanes] = x_seq.astype(bf16)
            wx = (x_seq * wide[0, :, lanes]).astype(bf16)
            first_added = mm(b0_t, wx[0:Q])
            added0[:, lanes] = first_added.astype(bf16)
            summary = first_added * wide[1, 2 * Q - 1 : 2 * Q, lanes] + mm(b1_t, wx[Q:])
            s_out[part] = summary.astype(bf16).reshape(team, owned, half)

            @pl.loop(1, team)
            def _(step):
                peer = lax.rem(place + step, team)
                remote(
                    s_out.at[part, peer],
                    s_in.at[layer, part, place],
                    s_send.at[part, step],
                    s_recv.at[layer, part, place],
                    base + peer,
                ).start()

            s_in[layer, part, place] = s_out[part, place]

        scores = [
            lax.dot_general(
                seq[k * Q : (k + 1) * Q, E + N :],
                seq[k * Q : (k + 1) * Q, E : E + N],
                (((1,), (1,)), ((), ())),
                preferred_element_type=f32,
            )
            for k in range(2)
        ]
        causal = iota((Q, Q), 0) >= iota((Q, Q), 1)
        low_lanes = iota((Q, 2 * P_SIZE), 1) < P_SIZE

        def pair_step(pair, carry):
            lanes = pl.ds(pl.multiple_of(pair * 2 * P_SIZE, 2 * P_SIZE), 2 * P_SIZE)
            for k in range(2):
                span = slice(k * Q, (k + 1) * Q)
                mixes = []
                for side in range(2):
                    row = lt[pair, side : side + 1, span]
                    step_row = dtt[pair, side : side + 1, span]
                    here = jnp.broadcast_to(row, (Q, Q))
                    decay = jnp.exp(jnp.where(causal, here.T - here, -1e30))
                    mixes.append((carry[k] * decay * step_row).astype(bf16))
                pair_x = seq[span, lanes].astype(f32)
                both = jnp.concatenate(
                    [jnp.where(low_lanes, pair_x, 0.0), jnp.where(low_lanes, 0.0, pair_x)], axis=0
                ).astype(bf16)
                y[span, lanes] = mm(jnp.concatenate(mixes, axis=1), both)
            return carry

        lax.fori_loop(0, PAIRS, pair_step, tuple(scores))

        @pl.loop(1, tiles)
        def _(step):
            source = lax.rem(me + tiles - step, tiles)
            remote(
                d_out, d_in.at[layer, source], d_send.at[step], d_recv.at[layer, source], left
            ).wait()

        pick = (iota((N, E), 0) == iota((N, E), 1) // P_SIZE).astype(f32).astype(bf16)
        high, low = split(d_in[layer].reshape(tiles * 8, N))
        d_wide[...] = (mm(high, pick) + mm(low, pick)).reshape(tiles, 8, E)

        def hand_back(part, tile):
            return remote(
                p_out.at[part, tile],
                p_in.at[layer, part, place],
                p_send.at[part, tile],
                p_recv.at[layer, part, place],
                base + tile,
            )

        def total_copy(part, to):
            return remote(
                t_out.at[part],
                t_in.at[layer, part, my_team],
                t_send.at[part, to],
                t_recv.at[layer, part, my_team],
                to * team + place,
            )

        def keep_back(part):
            p_in[layer, part, place] = p_out[part, place]

        for part in range(2):
            lanes = slice(part * half, (part + 1) * half)

            def tile_step(tile, carry):
                state, factor = carry
                rel[part, tile] = state
                factors[part, tile] = factor

                @pl.when(my_team == 0)
                def _():
                    p_out[part, tile] = state.astype(bf16)

                    @pl.when(tile != place)
                    def _():
                        hand_back(part, tile).start()

                @pl.when(tile != place)
                def _():
                    remote(
                        s_out.at[part, 0],
                        s_in.at[layer, part, tile],
                        s_send.at[part, 0],
                        s_recv.at[layer, part, tile],
                        left,
                    ).wait_recv()

                decay = d_wide[base + tile, :, lanes]
                return (
                    state * decay[0:1] + s_in[layer, part, tile].astype(f32),
                    factor * decay,
                )

            state, _ = lax.fori_loop(
                0, team, tile_step, (jnp.zeros((owned, half), f32), jnp.ones((8, half), f32))
            )
            t_out[part] = state.astype(bf16)

            @pl.loop(my_team + 1, teams)
            def _(to):
                total_copy(part, to).start()

        fetch_weight(5, layer).wait()
        gate = mm(normed_seq[...], gate_w[layer]).astype(bf16).astype(f32)
        gates[...] = gate * (1.0 / (1.0 + jnp.exp(-gate)))
        y[...] += skip_wide * seq[:, 0:E].astype(f32)
        y[Q:, :] += wide[1, Q:] * mm(seq[Q:, E + N :], added0[...])

        for part in range(2):
            lanes = slice(part * half, (part + 1) * half)

            @pl.when(my_team > 0)
            def _():
                def team_step(earlier, state):
                    remote(
                        t_out.at[part],
                        t_in.at[layer, part, earlier],
                        t_send.at[part, 0],
                        t_recv.at[layer, part, earlier],
                        left,
                    ).wait_recv()
                    decay = lax.fori_loop(
                        0,
                        team,
                        lambda tile, so_far: so_far * d_wide[earlier * team + tile, :, lanes],
                        jnp.ones((8, half), f32),
                    )
                    return state * decay[0:1] + t_in[layer, part, earlier].astype(f32)

                entering = lax.fori_loop(
                    0, my_team, team_step, jnp.zeros((owned, half), f32)
                )

                @pl.loop(0, team)
                def _(tile):
                    p_out[part, tile] = (
                        entering * factors[part, tile, 0:1, :] + rel[part, tile]
                    ).astype(bf16)

                    @pl.when(tile != place)
                    def _():
                        hand_back(part, tile).start()

            keep_back(part)

        maps_seq = seq[:, E + N :]
        for part in range(2):
            lanes = slice(part * half, (part + 1) * half)

            @pl.loop(1, team)
            def _(step):
                source = lax.rem(place + step, team)
                remote(
                    p_out.at[part, 0],
                    p_in.at[layer, part, source],
                    p_send.at[part, 0],
                    p_recv.at[layer, part, source],
                    left,
                ).wait_recv()

            y[:, lanes] += wide[2, :, lanes] * mm(maps_seq, p_in[layer, part].reshape(N, half))

        result = y[...]
        gated = result * gates[...]
        gated = (
            gated
            * lax.rsqrt(jnp.mean(gated * gated, axis=-1, keepdims=True) + epsilon)
            * of_layer(gain, layer)
        ).astype(bf16)
        fetch_weight(13, layer).wait()
        back = mm(perm_t[...], gated).astype(bf16)
        stream[...] = (stream[...] + mm(back, out_w[layer])).astype(bf16).astype(f32)

        to_left.wait_send()
        to_right.wait_send()

        for part in range(2):

            @pl.loop(1, team)
            def _(step):
                peer = lax.rem(place + step, team)
                remote(
                    s_out.at[part, peer],
                    s_in.at[layer, part, place],
                    s_send.at[part, step],
                    s_recv.at[layer, part, place],
                    base + peer,
                ).wait_send()
                hand_back(part, peer).wait_send()

            @pl.loop(my_team + 1, teams)
            def _(to):
                total_copy(part, to).wait_send()

    out[...] = stream[...].reshape(lat, across, channels).astype(bf16)


def shards(
    fields,
    order,
    resets,
    land,
    xbc_weight,
    gate_weight,
    step_weight,
    conv_weight,
    land_shift,
    rates,
    keeps,
    skip_gain,
    norm_gain,
    out_weight,
):
    tiles = lax.axis_size("lon")
    lat, across, channels = fields.shape
    cells = lat * across
    mapped_width = xbc_weight.shape[2]
    team = min(8, tiles)
    teams, owned, half = tiles // team, N // team, E // 2
    dma = pltpu.SemaphoreType.DMA
    vmem = pltpu.VMEM
    arrays = (
        fields,
        order,
        resets,
        land.T,
        xbc_weight,
        gate_weight,
        step_weight.transpose(0, 2, 1),
        conv_weight.transpose(1, 2, 0, 3),
        land_shift,
        rates,
        keeps,
        skip_gain,
        norm_gain,
        out_weight,
    )
    return pl.pallas_call(
        functools.partial(kernel, tiles, team),
        out_shape=jax.ShapeDtypeStruct(fields.shape, bf16),
        in_specs=[pl.BlockSpec(memory_space=pltpu.HBM)] * len(arrays),
        out_specs=pl.BlockSpec(memory_space=vmem),
        scratch_shapes=[vmem(array.shape, array.dtype) for array in arrays]
        + [
            dma((len(arrays),)),
            dma((3, LAYERS)),
            vmem((cells, channels), f32),
            vmem((cells, cells), bf16),
            vmem((cells, cells), bf16),
            vmem((cells, mapped_width), bf16),
            vmem((cells, mapped_width), bf16),
            vmem((cells, mapped_width), bf16),
            vmem((cells, channels), bf16),
            vmem((cells, E), f32),
            vmem((PAIRS, 2, cells), f32),
            vmem((PAIRS, 2, cells), f32),
            vmem((cells, E), f32),
            vmem((3, cells, E), f32),
            vmem((N, E), bf16),
            vmem((2, lat, mapped_width), bf16),
            vmem((LAYERS, 2, lat, mapped_width), bf16),
            vmem((2, team, owned, half), bf16),
            vmem((LAYERS, 2, team, owned, half), bf16),
            vmem((2, owned, half), bf16),
            vmem((LAYERS, 2, teams, owned, half), bf16),
            vmem((2, team, owned, half), f32),
            vmem((2, team, 8, half), f32),
            vmem((8, N), f32),
            vmem((LAYERS, tiles, 8, N), f32),
            vmem((tiles, 8, E), f32),
            vmem((2, team, owned, half), bf16),
            vmem((LAYERS, 2, team, owned, half), bf16),
            dma((2,)),
            dma((LAYERS, 2)),
            dma((2, team)),
            dma((LAYERS, 2, team)),
            dma((2, teams)),
            dma((LAYERS, 2, teams)),
            dma((tiles,)),
            dma((LAYERS, tiles)),
            dma((2, team)),
            dma((LAYERS, 2, team)),
        ],
        compiler_params=pltpu.CompilerParams(
            collective_id=0, has_side_effects=True, vmem_limit_bytes=60 * 1024 * 1024
        ),
        cost_estimate=pl.CostEstimate(
            flops=2 * 10**9, bytes_accessed=8 * 10**6, transcendentals=3 * 10**6
        ),
    )(*arrays)


def solution(mesh):
    return jax.shard_map(
        shards,
        mesh=mesh,
        in_specs=(
            P(None, ("groups", "lon"), None),
            P("lon", None),
            P("lon", None),
            P(None, "lon"),
            P(),
            P(),
            P(),
            P(),
            P(),
            P(),
            P(),
            P(),
            P(),
            P(),
        ),
        out_specs=P(None, ("groups", "lon"), None),
        check_vma=False,
    )
```

```python
import functools

import jax
import jax.numpy as jnp
from jax import lax
from jax.experimental import pallas as pl
from jax.experimental.pallas import tpu as pltpu
from jax.sharding import PartitionSpec as P

H = 16
P_SIZE = 64
N = 128
E = 1024
Q = 128
LAYERS = 2
PAIRS = H // 2

epsilon = 1e-05
bf16 = jnp.bfloat16
f32 = jnp.float32


def mm(a, b):
    return jnp.dot(a, b, preferred_element_type=f32)


def split(values):
    high = values.astype(bf16)
    low = (values - high.astype(f32)).astype(bf16)
    return high, low


def silu(x):
    return 0.5 * x * (1.0 + jnp.tanh(0.5 * x))


def of_layer(ref, layer):
    return jnp.where(layer == 0, ref[0:1], ref[1:2])


def iota(shape, dim):
    return lax.broadcasted_iota(jnp.int32, shape, dim)


def kernel(
    tiles,
    team,
    *refs,
):
    names = 14
    given, (out, *refs) = refs[:names], refs[names:]
    held, refs = refs[:names], refs[names:]
    (fields, order, resets, land, xbc_w, gate_w, step_w, conv_w) = held[:8]
    (shift, rates, keeps, skip, gain, out_w) = held[8:]
    (
    given_sem,
    weight_sem,
    stream,
    perm,
    perm_t,
    mapped,
    act,
    seq,
    normed_seq,
    gates,
    lt,
    dtt,
    y,
    wide,
    added0,
    halo_out,
    halo_in,
    s_out,
    s_in,
    t_out,
    t_in,
    rel,
    factors,
    g_out,
    g_in,
    d_out,
    d_in,
    d_wide,
    p_out,
    p_in,
    halo_send,
    halo_recv,
    s_send,
    s_recv,
    t_send,
    t_recv,
    g_send,
    g_recv,
    d_send,
    d_recv,
    p_send,
    p_recv,
    ) = refs
    lat, across, channels = fields.shape
    cells = lat * across
    teams = tiles // team
    half = E // 2
    owned = N // team
    me = lax.axis_index("lon")
    my_team, place = me // team, me % team
    base = my_team * team
    right, left = lax.rem(me + 1, tiles), lax.rem(me + tiles - 1, tiles)

    big = {4: 0, 5: 1, 13: 2}

    def fetch(index):
        return pltpu.make_async_copy(given[index], held[index], given_sem.at[index])

    def fetch_weight(index, layer):
        return pltpu.make_async_copy(
            given[index].at[layer], held[index].at[layer], weight_sem.at[big[index], layer]
        )

    small = [index for index in range(names) if index not in big]
    early = (0, 1, 2, 3)
    for index in early:
        fetch(index).start()
    fetch_weight(4, 0).start()
    for index in small:
        if index not in early:
            fetch(index).start()
    for index, layer in ((5, 0), (13, 0), (4, 1), (5, 1), (13, 1)):
        fetch_weight(index, layer).start()

    barrier = pltpu.get_barrier_semaphore()

    def greet(device):
        pl.semaphore_signal(
            barrier, inc=1, device_id={"lon": device}, device_id_type=pl.DeviceIdType.MESH
        )

    greet(left)
    greet(right)

    @pl.loop(1, team)
    def _(step):
        greet(base + lax.rem(place + step, team))

    @pl.loop(1, teams)
    def _(step):
        greet(lax.rem(my_team + step, teams) * team + place)

    for index in early:
        fetch(index).wait()
    perm_f = (order[...] == iota((cells, cells), 0)).astype(f32)
    perm_t[...] = perm_f.astype(bf16)
    perm_s = perm_f.T
    perm[...] = perm_s.astype(bf16)
    at_row = (iota((cells, lat), 0) // across == iota((cells, lat), 1)).astype(f32).astype(bf16)
    land_of = lax.dot_general(
        at_row,
        land[...].astype(f32).astype(bf16),
        (((1,), (1,)), ((), ())),
        preferred_element_type=f32,
    )
    on_column = iota((cells, across), 0) % across == iota((cells, across), 1)
    land_of = jnp.where(on_column, land_of, 0.0).astype(bf16)
    land_seq = jnp.sum(mm(perm[...], land_of), axis=1, keepdims=True)
    rows, cols = iota((cells, cells), 0), iota((cells, cells), 1)
    reset_col = jnp.sum(
        jnp.where(rows == cols, resets[...].astype(f32), 0.0), axis=1, keepdims=True
    )
    stream[...] = fields[...].astype(f32).reshape(cells, channels)

    for index in small:
        if index not in early:
            fetch(index).wait()

    def remote(src, dst, send, recv, peer):
        return pltpu.make_async_remote_copy(
            src_ref=src,
            dst_ref=dst,
            send_sem=send,
            recv_sem=recv,
            device_id={"lon": peer},
            device_id_type=pl.DeviceIdType.MESH,
        )

    @pl.loop(0, LAYERS)
    def _(layer):
        values = stream[...]
        norm = (
            values * lax.rsqrt(jnp.mean(values * values, axis=-1, keepdims=True) + epsilon)
        ).astype(bf16)
        fetch_weight(4, layer).wait()
        edge_rows, edge_cols = iota((2 * lat, cells), 0), iota((2 * lat, cells), 1)
        edge_cell = edge_rows * across + jnp.where(edge_rows < lat, 0, across - 1 - cells)
        edges = mm((edge_cols == edge_cell).astype(f32).astype(bf16), norm).astype(bf16)
        halo_out[...] = mm(edges, xbc_w[layer]).astype(bf16).reshape(2, lat, -1)

        @pl.when(layer == 0)
        def _():
            pl.semaphore_wait(barrier, team + teams)

        to_left = remote(
            halo_out.at[0], halo_in.at[layer, 1], halo_send.at[0], halo_recv.at[layer, 1], left
        )
        to_right = remote(
            halo_out.at[1], halo_in.at[layer, 0], halo_send.at[1], halo_recv.at[layer, 0], right
        )
        to_left.start()
        to_right.start()
        mapped[...] = mm(norm, xbc_w[layer]).astype(bf16)

        norm_seq = mm(perm[...], norm).astype(bf16)
        normed_seq[...] = norm_seq
        raw = lax.dot_general(
            norm_seq, step_w[layer], (((1,), (1,)), ((), ())), preferred_element_type=f32
        ) + land_seq * of_layer(shift, layer)
        dt = jnp.maximum(raw, 0.0) + jnp.log1p(jnp.exp(-jnp.abs(raw)))
        log_step = -of_layer(rates, layer) * dt + reset_col * jnp.log(of_layer(keeps, layer))
        lower = ((rows >= cols) & (rows // Q == cols // Q)).astype(f32)
        cum = jnp.dot(
            lower, log_step, precision=lax.Precision.HIGHEST, preferred_element_type=f32
        )
        cum0, cum1 = cum[Q - 1 : Q], cum[2 * Q - 1 : 2 * Q]
        second = iota((cells, H), 0) >= Q
        cum_t, dt_t = cum.T, dt.T
        for head in range(H):
            lt[head // 2, head % 2 : head % 2 + 1, :] = cum_t[head : head + 1]
            dtt[head // 2, head % 2 : head % 2 + 1, :] = dt_t[head : head + 1]
        d_out[...] = jnp.zeros_like(d_out)
        d_out[:, 0:H] = jnp.broadcast_to(jnp.exp(cum0 + cum1), (8, H))

        @pl.loop(1, team)
        def _(step):
            remote(
                d_out,
                d_in.at[layer, place],
                d_send.at[step],
                d_recv.at[layer, place],
                base + lax.rem(place + step, team),
            ).start()

        d_in[layer, place] = d_out[...]

        weight = jnp.exp(jnp.where(second, cum1, cum0) - cum) * dt
        since = jnp.exp(cum)
        since_tile = jnp.exp(jnp.where(second, cum + cum0, cum))
        spread = (iota((H, E), 0) == iota((H, E), 1) // P_SIZE).astype(f32).astype(bf16)
        for index, compact in enumerate((weight, since, since_tile)):
            high, low = split(compact)
            wide[index] = mm(high, spread) + mm(low, spread)
        skip_high, skip_low = split(jnp.broadcast_to(of_layer(skip, layer), (8, H)))
        skip_wide = (mm(skip_high, spread) + mm(skip_low, spread))[0:1]

        to_left.wait_recv()
        to_right.wait_recv()

        group = 256
        place_rows, place_cols = iota((cells, lat), 0), iota((cells, lat), 1)
        at_first = (place_rows == place_cols * across).astype(f32).astype(bf16)
        at_last = (place_rows == place_cols * across + across - 1).astype(f32).astype(bf16)

        def filter_part(part):
            lanes = pl.ds(pl.multiple_of(part * group, group), group)
            mid = mapped[:, lanes].astype(f32).reshape(lat, across, group)
            column = iota((lat, across, group), 1)
            before = jnp.where(column == 0, 0.0, pltpu.roll(mid, 1, 1)) + mm(
                at_first, halo_in[layer, 0, :, lanes]
            ).reshape(lat, across, group)
            after = jnp.where(column == across - 1, 0.0, pltpu.roll(mid, across - 1, 1)) + mm(
                at_last, halo_in[layer, 1, :, lanes]
            ).reshape(lat, across, group)
            total = None
            empty = jnp.zeros((1, across, group), f32)
            for row_off in range(3):
                line = None
                for col_off, moved in enumerate((before, mid, after)):
                    factor = jnp.where(
                        layer == 0,
                        conv_w[row_off, col_off, 0:1, lanes],
                        conv_w[row_off, col_off, 1:2, lanes],
                    )
                    term = moved * factor[None]
                    line = term if line is None else line + term
                if row_off == 0:
                    line = jnp.concatenate([empty, line[:-1]], axis=0)
                if row_off == 2:
                    line = jnp.concatenate([line[1:], empty], axis=0)
                total = line if total is None else total + line
            act[:, lanes] = (
                silu(total).reshape(cells, group).astype(bf16)
            )

        pl.loop(E // group, xbc_w.shape[2] // group)(filter_part)
        seq[:, E:] = mm(perm[...], act[:, E:]).astype(bf16)
        b0_t = seq[0:Q, E : E + N].astype(f32).T.astype(bf16)
        b1_t = seq[Q:, E : E + N].astype(f32).T.astype(bf16)

        for part in range(2):
            lanes = slice(part * half, (part + 1) * half)
            pl.loop(part * (half // group), (part + 1) * (half // group))(filter_part)
            x_seq = mm(perm[...], act[:, lanes])
            seq[:, lanes] = x_seq.astype(bf16)
            wx = (x_seq * wide[0, :, lanes]).astype(bf16)
            first_added = mm(b0_t, wx[0:Q])
            added0[:, lanes] = first_added.astype(bf16)
            summary = first_added * wide[1, 2 * Q - 1 : 2 * Q, lanes] + mm(b1_t, wx[Q:])
            s_out[part] = summary.astype(bf16).reshape(team, owned, half)

            @pl.loop(1, team)
            def _(step):
                peer = lax.rem(place + step, team)
                remote(
                    s_out.at[part, peer],
                    s_in.at[layer, part, place],
                    s_send.at[part, step],
                    s_recv.at[layer, part, place],
                    base + peer,
                ).start()

            s_in[layer, part, place] = s_out[part, place]

        scores = [
            lax.dot_general(
                seq[k * Q : (k + 1) * Q, E + N :],
                seq[k * Q : (k + 1) * Q, E : E + N],
                (((1,), (1,)), ((), ())),
                preferred_element_type=f32,
            )
            for k in range(2)
        ]
        causal = iota((Q, Q), 0) >= iota((Q, Q), 1)
        low_lanes = iota((Q, 2 * P_SIZE), 1) < P_SIZE

        def pair_step(pair, carry):
            lanes = pl.ds(pl.multiple_of(pair * 2 * P_SIZE, 2 * P_SIZE), 2 * P_SIZE)
            for k in range(2):
                span = slice(k * Q, (k + 1) * Q)
                mixes = []
                for side in range(2):
                    row = lt[pair, side : side + 1, span]
                    step_row = dtt[pair, side : side + 1, span]
                    here = jnp.broadcast_to(row, (Q, Q))
                    decay = jnp.exp(jnp.where(causal, here.T - here, -1e30))
                    mixes.append((carry[k] * decay * step_row).astype(bf16))
                pair_x = seq[span, lanes].astype(f32)
                both = jnp.concatenate(
                    [jnp.where(low_lanes, pair_x, 0.0), jnp.where(low_lanes, 0.0, pair_x)], axis=0
                ).astype(bf16)
                y[span, lanes] = mm(jnp.concatenate(mixes, axis=1), both)
            return carry

        lax.fori_loop(0, PAIRS, pair_step, tuple(scores))

        @pl.loop(1, team)
        def _(step):
            source = lax.rem(place + team - step, team)
            remote(
                d_out, d_in.at[layer, source], d_send.at[step], d_recv.at[layer, source], left
            ).wait()

        pick = (iota((N, E), 0) == iota((N, E), 1) // P_SIZE).astype(f32).astype(bf16)
        high, low = split(d_in[layer].reshape(team * 8, N))
        d_wide[...] = (mm(high, pick) + mm(low, pick)).reshape(team, 8, E)

        def hand_back(part, tile):
            return remote(
                p_out.at[part, tile],
                p_in.at[layer, part, place],
                p_send.at[part, tile],
                p_recv.at[layer, part, place],
                base + tile,
            )

        def total_copy(part, to):
            return remote(
                t_out.at[part],
                t_in.at[layer, part, my_team],
                t_send.at[part, to],
                t_recv.at[layer, part, my_team],
                to * team + place,
            )

        def decay_copy(to):
            return remote(
                g_out,
                g_in.at[layer, my_team],
                g_send.at[to],
                g_recv.at[layer, my_team],
                to * team + place,
            )

        if teams > 2:
            g_out[...] = functools.reduce(
                lambda a, b: a * b, [d_in[layer, tile] for tile in range(team)]
            )

            @pl.loop(my_team + 1, teams)
            def _(to):
                decay_copy(to).start()

            @pl.loop(0, my_team)
            def _(earlier):
                remote(
                    g_out, g_in.at[layer, earlier], g_send.at[0], g_recv.at[layer, earlier], left
                ).wait_recv()

        def keep_back(part):
            p_in[layer, part, place] = p_out[part, place]

        for part in range(2):
            lanes = slice(part * half, (part + 1) * half)

            def tile_step(tile, carry):
                state, factor = carry
                rel[part, tile] = state
                factors[part, tile] = factor

                @pl.when(tile != place)
                def _():
                    remote(
                        s_out.at[part, 0],
                        s_in.at[layer, part, tile],
                        s_send.at[part, 0],
                        s_recv.at[layer, part, tile],
                        left,
                    ).wait_recv()

                decay = d_wide[tile, :, lanes]
                return (
                    state * decay[0:1] + s_in[layer, part, tile].astype(f32),
                    factor * decay,
                )

            state, _ = lax.fori_loop(
                0, team, tile_step, (jnp.zeros((owned, half), f32), jnp.ones((8, half), f32))
            )
            t_out[part] = state.astype(bf16)

            @pl.loop(my_team + 1, teams)
            def _(to):
                total_copy(part, to).start()

            @pl.when(my_team == 0)
            def _():
                @pl.loop(0, team)
                def _(tile):
                    p_out[part, tile] = rel[part, tile].astype(bf16)

                    @pl.when(tile != place)
                    def _():
                        hand_back(part, tile).start()

        fetch_weight(5, layer).wait()
        gate = mm(normed_seq[...], gate_w[layer]).astype(bf16).astype(f32)
        gates[...] = silu(gate)
        y[...] += skip_wide * seq[:, 0:E].astype(f32)
        y[Q:, :] += wide[1, Q:] * mm(seq[Q:, E + N :], added0[...])

        for part in range(2):
            lanes = slice(part * half, (part + 1) * half)

            @pl.when(my_team > 0)
            def _():
                def team_step(earlier, state):
                    remote(
                        t_out.at[part],
                        t_in.at[layer, part, earlier],
                        t_send.at[part, 0],
                        t_recv.at[layer, part, earlier],
                        left,
                    ).wait_recv()
                    total = t_in[layer, part, earlier].astype(f32)
                    if teams == 2:
                        return total
                    high, low = split(g_in[layer, earlier])
                    decay = mm(high, pick[:, lanes]) + mm(low, pick[:, lanes])
                    return state * decay[0:1] + total

                entering = lax.fori_loop(
                    0, my_team, team_step, jnp.zeros((owned, half), f32)
                )

                @pl.loop(0, team)
                def _(tile):
                    p_out[part, tile] = (
                        entering * factors[part, tile, 0:1, :] + rel[part, tile]
                    ).astype(bf16)

                    @pl.when(tile != place)
                    def _():
                        hand_back(part, tile).start()

            keep_back(part)

        maps_seq = seq[:, E + N :]
        for part in range(2):
            lanes = slice(part * half, (part + 1) * half)

            @pl.loop(1, team)
            def _(step):
                source = lax.rem(place + step, team)
                remote(
                    p_out.at[part, 0],
                    p_in.at[layer, part, source],
                    p_send.at[part, 0],
                    p_recv.at[layer, part, source],
                    left,
                ).wait_recv()

            y[:, lanes] += wide[2, :, lanes] * mm(maps_seq, p_in[layer, part].reshape(N, half))

        result = y[...]
        gated = result * gates[...]
        gated = (
            gated
            * lax.rsqrt(jnp.mean(gated * gated, axis=-1, keepdims=True) + epsilon)
            * of_layer(gain, layer)
        ).astype(bf16)
        fetch_weight(13, layer).wait()
        back = mm(perm_t[...], gated).astype(bf16)
        stream[...] = (stream[...] + mm(back, out_w[layer])).astype(bf16).astype(f32)

        to_left.wait_send()
        to_right.wait_send()

        if teams > 2:

            @pl.loop(my_team + 1, teams)
            def _(to):
                decay_copy(to).wait_send()

        for part in range(2):

            @pl.loop(1, team)
            def _(step):
                peer = lax.rem(place + step, team)
                remote(
                    s_out.at[part, peer],
                    s_in.at[layer, part, place],
                    s_send.at[part, step],
                    s_recv.at[layer, part, place],
                    base + peer,
                ).wait_send()
                hand_back(part, peer).wait_send()

            @pl.loop(my_team + 1, teams)
            def _(to):
                total_copy(part, to).wait_send()

    out[...] = stream[...].reshape(lat, across, channels).astype(bf16)


def shards(
    fields,
    order,
    resets,
    land,
    xbc_weight,
    gate_weight,
    step_weight,
    conv_weight,
    land_shift,
    rates,
    keeps,
    skip_gain,
    norm_gain,
    out_weight,
):
    tiles = lax.axis_size("lon")
    lat, across, channels = fields.shape
    cells = lat * across
    mapped_width = xbc_weight.shape[2]
    team = min(8, tiles)
    teams, owned, half = tiles // team, N // team, E // 2
    dma = pltpu.SemaphoreType.DMA
    vmem = pltpu.VMEM
    arrays = (
        fields,
        order,
        resets,
        land.T,
        xbc_weight,
        gate_weight,
        step_weight.transpose(0, 2, 1),
        conv_weight.transpose(1, 2, 0, 3),
        land_shift,
        rates,
        keeps,
        skip_gain,
        norm_gain,
        out_weight,
    )
    return pl.pallas_call(
        functools.partial(kernel, tiles, team),
        out_shape=jax.ShapeDtypeStruct(fields.shape, bf16),
        in_specs=[pl.BlockSpec(memory_space=pltpu.HBM)] * len(arrays),
        out_specs=pl.BlockSpec(memory_space=vmem),
        scratch_shapes=[vmem(array.shape, array.dtype) for array in arrays]
        + [
            dma((len(arrays),)),
            dma((3, LAYERS)),
            vmem((cells, channels), f32),
            vmem((cells, cells), bf16),
            vmem((cells, cells), bf16),
            vmem((cells, mapped_width), bf16),
            vmem((cells, mapped_width), bf16),
            vmem((cells, mapped_width), bf16),
            vmem((cells, channels), bf16),
            vmem((cells, E), f32),
            vmem((PAIRS, 2, cells), f32),
            vmem((PAIRS, 2, cells), f32),
            vmem((cells, E), f32),
            vmem((3, cells, E), f32),
            vmem((N, E), bf16),
            vmem((2, lat, mapped_width), bf16),
            vmem((LAYERS, 2, lat, mapped_width), bf16),
            vmem((2, team, owned, half), bf16),
            vmem((LAYERS, 2, team, owned, half), bf16),
            vmem((2, owned, half), bf16),
            vmem((LAYERS, 2, teams, owned, half), bf16),
            vmem((2, team, owned, half), f32),
            vmem((2, team, 8, half), f32),
            vmem((8, N), f32),
            vmem((LAYERS, teams, 8, N), f32),
            vmem((8, N), f32),
            vmem((LAYERS, team, 8, N), f32),
            vmem((team, 8, E), f32),
            vmem((2, team, owned, half), bf16),
            vmem((LAYERS, 2, team, owned, half), bf16),
            dma((2,)),
            dma((LAYERS, 2)),
            dma((2, team)),
            dma((LAYERS, 2, team)),
            dma((2, teams)),
            dma((LAYERS, 2, teams)),
            dma((teams,)),
            dma((LAYERS, teams)),
            dma((team,)),
            dma((LAYERS, team)),
            dma((2, team)),
            dma((LAYERS, 2, team)),
        ],
        compiler_params=pltpu.CompilerParams(
            collective_id=0, has_side_effects=True, vmem_limit_bytes=60 * 1024 * 1024
        ),
        cost_estimate=pl.CostEstimate(
            flops=2 * 10**9, bytes_accessed=8 * 10**6, transcendentals=3 * 10**6
        ),
    )(*arrays)


def solution(mesh):
    return jax.shard_map(
        shards,
        mesh=mesh,
        in_specs=(
            P(None, ("groups", "lon"), None),
            P("lon", None),
            P("lon", None),
            P(None, "lon"),
            P(),
            P(),
            P(),
            P(),
            P(),
            P(),
            P(),
            P(),
            P(),
            P(),
        ),
        out_specs=P(None, ("groups", "lon"), None),
        check_vma=False,
    )
```

```python
import functools

import jax
import jax.numpy as jnp
from jax import lax
from jax.experimental import pallas as pl
from jax.experimental.pallas import tpu as pltpu
from jax.sharding import PartitionSpec as P

H = 16
P_SIZE = 64
N = 128
E = 1024
Q = 128
LAYERS = 2
PAIRS = H // 2

epsilon = 1e-05
bf16 = jnp.bfloat16
f32 = jnp.float32


def mm(a, b):
    return jnp.dot(a, b, preferred_element_type=f32)


def split(values):
    high = values.astype(bf16)
    low = (values - high.astype(f32)).astype(bf16)
    return high, low


def silu(x):
    return 0.5 * x * (1.0 + jnp.tanh(0.5 * x))


def of_layer(ref, layer):
    return jnp.where(layer == 0, ref[0:1], ref[1:2])


def iota(shape, dim):
    return lax.broadcasted_iota(jnp.int32, shape, dim)


def kernel(
    tiles,
    team,
    *refs,
):
    names = 14
    given, (out, *refs) = refs[:names], refs[names:]
    held, refs = refs[:names], refs[names:]
    (fields, order, resets, land, xbc_w, gate_w, step_w, conv_w) = held[:8]
    (shift, rates, keeps, skip, gain, out_w) = held[8:]
    (
    given_sem,
    weight_sem,
    stream,
    perm,
    perm_t,
    mapped,
    own_sum,
    act,
    seq,
    normed_seq,
    lt,
    dtt,
    y,
    wide,
    added0,
    halo_out,
    halo_in,
    s_out,
    s_in,
    t_out,
    t_in,
    rel,
    factors,
    g_out,
    g_in,
    d_out,
    d_in,
    d_wide,
    p_out,
    p_in,
    halo_send,
    halo_recv,
    s_send,
    s_recv,
    t_send,
    t_recv,
    g_send,
    g_recv,
    d_send,
    d_recv,
    p_send,
    p_recv,
    ) = refs
    lat, across, channels = fields.shape
    cells = lat * across
    teams = tiles // team
    half = E // 2
    owned = N // team
    me = lax.axis_index("lon")
    my_team, place = me // team, me % team
    base = my_team * team
    right, left = lax.rem(me + 1, tiles), lax.rem(me + tiles - 1, tiles)

    big = {4: 0, 5: 1, 13: 2}

    def fetch(index):
        return pltpu.make_async_copy(given[index], held[index], given_sem.at[index])

    def fetch_weight(index, layer):
        return pltpu.make_async_copy(
            given[index].at[layer], held[index].at[layer], weight_sem.at[big[index], layer]
        )

    small = [index for index in range(names) if index not in big]
    early = (0, 1, 2, 3)
    for index in early:
        fetch(index).start()
    fetch_weight(4, 0).start()
    for index in small:
        if index not in early:
            fetch(index).start()
    for index, layer in ((5, 0), (13, 0), (4, 1), (5, 1), (13, 1)):
        fetch_weight(index, layer).start()

    barrier = pltpu.get_barrier_semaphore()

    def greet(device):
        pl.semaphore_signal(
            barrier, inc=1, device_id={"lon": device}, device_id_type=pl.DeviceIdType.MESH
        )

    greet(left)
    greet(right)

    @pl.loop(1, team)
    def _(step):
        greet(base + lax.rem(place + step, team))

    @pl.loop(1, teams)
    def _(step):
        greet(lax.rem(my_team + step, teams) * team + place)

    for index in early:
        fetch(index).wait()
    perm_f = (order[...] == iota((cells, cells), 0)).astype(f32)
    perm_t[...] = perm_f.astype(bf16)
    perm_s = perm_f.T
    perm[...] = perm_s.astype(bf16)
    at_row = (iota((cells, lat), 0) // across == iota((cells, lat), 1)).astype(f32).astype(bf16)
    land_of = lax.dot_general(
        at_row,
        land[...].astype(f32).astype(bf16),
        (((1,), (1,)), ((), ())),
        preferred_element_type=f32,
    )
    on_column = iota((cells, across), 0) % across == iota((cells, across), 1)
    land_of = jnp.where(on_column, land_of, 0.0).astype(bf16)
    land_seq = jnp.sum(mm(perm[...], land_of), axis=1, keepdims=True)
    rows, cols = iota((cells, cells), 0), iota((cells, cells), 1)
    reset_col = jnp.sum(
        jnp.where(rows == cols, resets[...].astype(f32), 0.0), axis=1, keepdims=True
    )
    stream[...] = fields[...].astype(f32).reshape(cells, channels)

    for index in small:
        if index not in early:
            fetch(index).wait()

    def remote(src, dst, send, recv, peer):
        return pltpu.make_async_remote_copy(
            src_ref=src,
            dst_ref=dst,
            send_sem=send,
            recv_sem=recv,
            device_id={"lon": peer},
            device_id_type=pl.DeviceIdType.MESH,
        )

    @pl.loop(0, LAYERS)
    def _(layer):
        values = stream[...]
        norm = (
            values * lax.rsqrt(jnp.mean(values * values, axis=-1, keepdims=True) + epsilon)
        ).astype(bf16)
        fetch_weight(4, layer).wait()
        edge_rows, edge_cols = iota((2 * lat, cells), 0), iota((2 * lat, cells), 1)
        edge_cell = edge_rows * across + jnp.where(edge_rows < lat, 0, across - 1 - cells)
        edges = mm((edge_cols == edge_cell).astype(f32).astype(bf16), norm).astype(bf16)
        halo_out[...] = mm(edges, xbc_w[layer]).astype(bf16).reshape(2, lat, -1)

        @pl.when(layer == 0)
        def _():
            pl.semaphore_wait(barrier, team + teams)

        to_left = remote(
            halo_out.at[0], halo_in.at[layer, 1], halo_send.at[0], halo_recv.at[layer, 1], left
        )
        to_right = remote(
            halo_out.at[1], halo_in.at[layer, 0], halo_send.at[1], halo_recv.at[layer, 0], right
        )
        to_left.start()
        to_right.start()
        mapped[...] = mm(norm, xbc_w[layer]).astype(bf16)

        norm_seq = mm(perm[...], norm).astype(bf16)
        normed_seq[...] = norm_seq
        raw = lax.dot_general(
            norm_seq, step_w[layer], (((1,), (1,)), ((), ())), preferred_element_type=f32
        ) + land_seq * of_layer(shift, layer)
        dt = jnp.maximum(raw, 0.0) + jnp.log1p(jnp.exp(-jnp.abs(raw)))
        log_step = -of_layer(rates, layer) * dt + reset_col * jnp.log(of_layer(keeps, layer))
        lower = ((rows >= cols) & (rows // Q == cols // Q)).astype(f32)
        cum = jnp.dot(
            lower, log_step, precision=lax.Precision.HIGHEST, preferred_element_type=f32
        )
        cum0, cum1 = cum[Q - 1 : Q], cum[2 * Q - 1 : 2 * Q]
        second = iota((cells, H), 0) >= Q
        cum_t, dt_t = cum.T, dt.T
        for head in range(H):
            lt[head // 2, head % 2 : head % 2 + 1, :] = cum_t[head : head + 1]
            dtt[head // 2, head % 2 : head % 2 + 1, :] = dt_t[head : head + 1]
        d_out[...] = jnp.zeros_like(d_out)
        d_out[:, 0:H] = jnp.broadcast_to(jnp.exp(cum0 + cum1), (8, H))

        @pl.loop(1, team)
        def _(step):
            remote(
                d_out,
                d_in.at[layer, place],
                d_send.at[step],
                d_recv.at[layer, place],
                base + lax.rem(place + step, team),
            ).start()

        d_in[layer, place] = d_out[...]

        weight = jnp.exp(jnp.where(second, cum1, cum0) - cum) * dt
        since = jnp.exp(cum)
        since_tile = jnp.exp(jnp.where(second, cum + cum0, cum))
        spread = (iota((H, E), 0) == iota((H, E), 1) // P_SIZE).astype(f32).astype(bf16)
        for index, compact in enumerate((weight, since, since_tile)):
            high, low = split(compact)
            wide[index] = mm(high, spread) + mm(low, spread)
        skip_high, skip_low = split(jnp.broadcast_to(of_layer(skip, layer), (8, H)))
        skip_wide = (mm(skip_high, spread) + mm(skip_low, spread))[0:1]

        group = 256

        def taps(row_off, col_off, lanes):
            return jnp.where(
                layer == 0,
                conv_w[row_off, col_off, 0:1, lanes],
                conv_w[row_off, col_off, 1:2, lanes],
            )

        @pl.loop(0, xbc_w.shape[2] // group)
        def _(part):
            lanes = pl.ds(pl.multiple_of(part * group, group), group)
            mid = mapped[:, lanes].astype(f32).reshape(lat, across, group)
            column = iota((lat, across, group), 1)
            before = jnp.where(column == 0, 0.0, pltpu.roll(mid, 1, 1))
            after = jnp.where(column == across - 1, 0.0, pltpu.roll(mid, across - 1, 1))
            total = None
            empty = jnp.zeros((1, across, group), f32)
            for row_off in range(3):
                line = None
                for col_off, moved in enumerate((before, mid, after)):
                    term = moved * taps(row_off, col_off, lanes)[None]
                    line = term if line is None else line + term
                if row_off == 0:
                    line = jnp.concatenate([empty, line[:-1]], axis=0)
                if row_off == 2:
                    line = jnp.concatenate([line[1:], empty], axis=0)
                total = line if total is None else total + line
            own_sum[:, lanes] = total.reshape(cells, group)

        to_left.wait_recv()
        to_right.wait_recv()

        place_rows, place_cols = iota((cells, 4 * lat), 0), iota((cells, 4 * lat), 1)
        target = place_cols % lat * across + jnp.where(place_cols < 2 * lat, 0, across - 1)
        at_edges = (place_rows == target).astype(f32).astype(bf16)

        def filter_part(part):
            lanes = pl.ds(pl.multiple_of(part * group, group), group)
            line_row = iota((lat, group), 0)
            terms = []
            for side in range(2):
                edge = halo_in[layer, side, :, lanes].astype(f32)
                above = jnp.where(line_row == 0, 0.0, pltpu.roll(edge, 1, 0))
                below = jnp.where(line_row == lat - 1, 0.0, pltpu.roll(edge, lat - 1, 0))
                terms.extend(
                    split(
                        above * taps(0, 2 * side, lanes)
                        + edge * taps(1, 2 * side, lanes)
                        + below * taps(2, 2 * side, lanes)
                    )
                )
            total = own_sum[:, lanes] + mm(at_edges, jnp.concatenate(terms, axis=0))
            act[:, lanes] = silu(total).astype(bf16)

        pl.loop(E // group, xbc_w.shape[2] // group)(filter_part)
        seq[:, E:] = mm(perm[...], act[:, E:]).astype(bf16)
        b0_t = seq[0:Q, E : E + N].astype(f32).T.astype(bf16)
        b1_t = seq[Q:, E : E + N].astype(f32).T.astype(bf16)

        for part in range(2):
            lanes = slice(part * half, (part + 1) * half)
            pl.loop(part * (half // group), (part + 1) * (half // group))(filter_part)
            x_seq = mm(perm[...], act[:, lanes])
            seq[:, lanes] = x_seq.astype(bf16)
            wx = (x_seq * wide[0, :, lanes]).astype(bf16)
            first_added = mm(b0_t, wx[0:Q])
            added0[:, lanes] = first_added.astype(bf16)
            summary = first_added * wide[1, 2 * Q - 1 : 2 * Q, lanes] + mm(b1_t, wx[Q:])
            s_out[part] = summary.astype(bf16).reshape(team, owned, half)

            @pl.loop(1, team)
            def _(step):
                peer = lax.rem(place + step, team)
                remote(
                    s_out.at[part, peer],
                    s_in.at[layer, part, place],
                    s_send.at[part, step],
                    s_recv.at[layer, part, place],
                    base + peer,
                ).start()

            s_in[layer, part, place] = s_out[part, place]

        scores = [
            lax.dot_general(
                seq[k * Q : (k + 1) * Q, E + N :],
                seq[k * Q : (k + 1) * Q, E : E + N],
                (((1,), (1,)), ((), ())),
                preferred_element_type=f32,
            )
            for k in range(2)
        ]
        causal = iota((Q, Q), 0) >= iota((Q, Q), 1)
        low_lanes = iota((Q, 2 * P_SIZE), 1) < P_SIZE

        def pair_step(pair, carry):
            lanes = pl.ds(pl.multiple_of(pair * 2 * P_SIZE, 2 * P_SIZE), 2 * P_SIZE)
            for k in range(2):
                span = slice(k * Q, (k + 1) * Q)
                mixes = []
                for side in range(2):
                    row = lt[pair, side : side + 1, span]
                    step_row = dtt[pair, side : side + 1, span]
                    here = jnp.broadcast_to(row, (Q, Q))
                    decay = jnp.exp(jnp.where(causal, here.T - here, -1e30))
                    mixes.append((carry[k] * decay * step_row).astype(bf16))
                pair_x = seq[span, lanes].astype(f32)
                both = jnp.concatenate(
                    [jnp.where(low_lanes, pair_x, 0.0), jnp.where(low_lanes, 0.0, pair_x)], axis=0
                ).astype(bf16)
                y[span, lanes] = mm(jnp.concatenate(mixes, axis=1), both)
            return carry

        lax.fori_loop(0, PAIRS, pair_step, tuple(scores))

        @pl.loop(1, team)
        def _(step):
            source = lax.rem(place + team - step, team)
            remote(
                d_out, d_in.at[layer, source], d_send.at[step], d_recv.at[layer, source], left
            ).wait()

        pick = (iota((N, E), 0) == iota((N, E), 1) // P_SIZE).astype(f32).astype(bf16)
        high, low = split(d_in[layer].reshape(team * 8, N))
        d_wide[...] = (mm(high, pick) + mm(low, pick)).reshape(team, 8, E)

        def hand_back(part, tile):
            return remote(
                p_out.at[part, tile],
                p_in.at[layer, part, place],
                p_send.at[part, tile],
                p_recv.at[layer, part, place],
                base + tile,
            )

        def total_copy(part, to):
            return remote(
                t_out.at[part],
                t_in.at[layer, part, my_team],
                t_send.at[part, to],
                t_recv.at[layer, part, my_team],
                to * team + place,
            )

        def decay_copy(to):
            return remote(
                g_out,
                g_in.at[layer, my_team],
                g_send.at[to],
                g_recv.at[layer, my_team],
                to * team + place,
            )

        if teams > 2:
            g_out[...] = functools.reduce(
                lambda a, b: a * b, [d_in[layer, tile] for tile in range(team)]
            )

            @pl.loop(my_team + 1, teams)
            def _(to):
                decay_copy(to).start()

            @pl.loop(0, my_team)
            def _(earlier):
                remote(
                    g_out, g_in.at[layer, earlier], g_send.at[0], g_recv.at[layer, earlier], left
                ).wait_recv()

        def keep_back(part):
            p_in[layer, part, place] = p_out[part, place]

        for part in range(2):
            lanes = slice(part * half, (part + 1) * half)

            def tile_step(tile, carry):
                state, factor = carry
                rel[part, tile] = state
                factors[part, tile] = factor

                @pl.when(tile != place)
                def _():
                    remote(
                        s_out.at[part, 0],
                        s_in.at[layer, part, tile],
                        s_send.at[part, 0],
                        s_recv.at[layer, part, tile],
                        left,
                    ).wait_recv()

                decay = d_wide[tile, :, lanes]
                return (
                    state * decay[0:1] + s_in[layer, part, tile].astype(f32),
                    factor * decay,
                )

            state, _ = lax.fori_loop(
                0, team, tile_step, (jnp.zeros((owned, half), f32), jnp.ones((8, half), f32))
            )
            t_out[part] = state.astype(bf16)

            @pl.loop(my_team + 1, teams)
            def _(to):
                total_copy(part, to).start()

            @pl.when(my_team == 0)
            def _():
                @pl.loop(0, team)
                def _(tile):
                    p_out[part, tile] = rel[part, tile].astype(bf16)

                    @pl.when(tile != place)
                    def _():
                        hand_back(part, tile).start()

        fetch_weight(5, layer).wait()
        gate = mm(normed_seq[...], gate_w[layer]).astype(bf16).astype(f32)
        gate = silu(gate)
        wide[2] = wide[2] * gate
        y[0:Q, :] = (y[0:Q, :] + skip_wide * seq[0:Q, 0:E].astype(f32)) * gate[0:Q]
        y[Q:, :] = (
            y[Q:, :]
            + skip_wide * seq[Q:, 0:E].astype(f32)
            + wide[1, Q:] * mm(seq[Q:, E + N :], added0[...])
        ) * gate[Q:]

        for part in range(2):
            lanes = slice(part * half, (part + 1) * half)

            @pl.when(my_team > 0)
            def _():
                def team_step(earlier, state):
                    remote(
                        t_out.at[part],
                        t_in.at[layer, part, earlier],
                        t_send.at[part, 0],
                        t_recv.at[layer, part, earlier],
                        left,
                    ).wait_recv()
                    total = t_in[layer, part, earlier].astype(f32)
                    if teams == 2:
                        return total
                    high, low = split(g_in[layer, earlier])
                    decay = mm(high, pick[:, lanes]) + mm(low, pick[:, lanes])
                    return state * decay[0:1] + total

                entering = lax.fori_loop(
                    0, my_team, team_step, jnp.zeros((owned, half), f32)
                )

                @pl.loop(0, team)
                def _(tile):
                    p_out[part, tile] = (
                        entering * factors[part, tile, 0:1, :] + rel[part, tile]
                    ).astype(bf16)

                    @pl.when(tile != place)
                    def _():
                        hand_back(part, tile).start()

            keep_back(part)

        maps_seq = seq[:, E + N :]
        for part in range(2):
            lanes = slice(part * half, (part + 1) * half)

            @pl.loop(1, team)
            def _(step):
                source = lax.rem(place + step, team)
                remote(
                    p_out.at[part, 0],
                    p_in.at[layer, part, source],
                    p_send.at[part, 0],
                    p_recv.at[layer, part, source],
                    left,
                ).wait_recv()

            y[:, lanes] += wide[2, :, lanes] * mm(maps_seq, p_in[layer, part].reshape(N, half))

        gated = y[...]
        gated = (
            gated
            * lax.rsqrt(jnp.mean(gated * gated, axis=-1, keepdims=True) + epsilon)
            * of_layer(gain, layer)
        ).astype(bf16)
        fetch_weight(13, layer).wait()
        back = mm(perm_t[...], gated).astype(bf16)
        stream[...] = (stream[...] + mm(back, out_w[layer])).astype(bf16).astype(f32)

        to_left.wait_send()
        to_right.wait_send()

        if teams > 2:

            @pl.loop(my_team + 1, teams)
            def _(to):
                decay_copy(to).wait_send()

        for part in range(2):

            @pl.loop(1, team)
            def _(step):
                peer = lax.rem(place + step, team)
                remote(
                    s_out.at[part, peer],
                    s_in.at[layer, part, place],
                    s_send.at[part, step],
                    s_recv.at[layer, part, place],
                    base + peer,
                ).wait_send()
                hand_back(part, peer).wait_send()

            @pl.loop(my_team + 1, teams)
            def _(to):
                total_copy(part, to).wait_send()

    out[...] = stream[...].reshape(lat, across, channels).astype(bf16)


def shards(
    fields,
    order,
    resets,
    land,
    xbc_weight,
    gate_weight,
    step_weight,
    conv_weight,
    land_shift,
    rates,
    keeps,
    skip_gain,
    norm_gain,
    out_weight,
):
    tiles = lax.axis_size("lon")
    lat, across, channels = fields.shape
    cells = lat * across
    mapped_width = xbc_weight.shape[2]
    team = min(8, tiles)
    teams, owned, half = tiles // team, N // team, E // 2
    dma = pltpu.SemaphoreType.DMA
    vmem = pltpu.VMEM
    arrays = (
        fields,
        order,
        resets,
        land.T,
        xbc_weight,
        gate_weight,
        step_weight.transpose(0, 2, 1),
        conv_weight.transpose(1, 2, 0, 3),
        land_shift,
        rates,
        keeps,
        skip_gain,
        norm_gain,
        out_weight,
    )
    return pl.pallas_call(
        functools.partial(kernel, tiles, team),
        out_shape=jax.ShapeDtypeStruct(fields.shape, bf16),
        in_specs=[pl.BlockSpec(memory_space=pltpu.HBM)] * len(arrays),
        out_specs=pl.BlockSpec(memory_space=vmem),
        scratch_shapes=[vmem(array.shape, array.dtype) for array in arrays]
        + [
            dma((len(arrays),)),
            dma((3, LAYERS)),
            vmem((cells, channels), f32),
            vmem((cells, cells), bf16),
            vmem((cells, cells), bf16),
            vmem((cells, mapped_width), bf16),
            vmem((cells, mapped_width), f32),
            vmem((cells, mapped_width), bf16),
            vmem((cells, mapped_width), bf16),
            vmem((cells, channels), bf16),
            vmem((PAIRS, 2, cells), f32),
            vmem((PAIRS, 2, cells), f32),
            vmem((cells, E), f32),
            vmem((3, cells, E), f32),
            vmem((N, E), bf16),
            vmem((2, lat, mapped_width), bf16),
            vmem((LAYERS, 2, lat, mapped_width), bf16),
            vmem((2, team, owned, half), bf16),
            vmem((LAYERS, 2, team, owned, half), bf16),
            vmem((2, owned, half), bf16),
            vmem((LAYERS, 2, teams, owned, half), bf16),
            vmem((2, team, owned, half), f32),
            vmem((2, team, 8, half), f32),
            vmem((8, N), f32),
            vmem((LAYERS, teams, 8, N), f32),
            vmem((8, N), f32),
            vmem((LAYERS, team, 8, N), f32),
            vmem((team, 8, E), f32),
            vmem((2, team, owned, half), bf16),
            vmem((LAYERS, 2, team, owned, half), bf16),
            dma((2,)),
            dma((LAYERS, 2)),
            dma((2, team)),
            dma((LAYERS, 2, team)),
            dma((2, teams)),
            dma((LAYERS, 2, teams)),
            dma((teams,)),
            dma((LAYERS, teams)),
            dma((team,)),
            dma((LAYERS, team)),
            dma((2, team)),
            dma((LAYERS, 2, team)),
        ],
        compiler_params=pltpu.CompilerParams(
            collective_id=0, has_side_effects=True, vmem_limit_bytes=60 * 1024 * 1024
        ),
        cost_estimate=pl.CostEstimate(
            flops=2 * 10**9, bytes_accessed=8 * 10**6, transcendentals=3 * 10**6
        ),
    )(*arrays)


def solution(mesh):
    return jax.shard_map(
        shards,
        mesh=mesh,
        in_specs=(
            P(None, ("groups", "lon"), None),
            P("lon", None),
            P("lon", None),
            P(None, "lon"),
            P(),
            P(),
            P(),
            P(),
            P(),
            P(),
            P(),
            P(),
            P(),
            P(),
        ),
        out_specs=P(None, ("groups", "lon"), None),
        check_vma=False,
    )
```
